768 devices in a mesh: seg: 96 (over z, x, core), sub: 8 (over y).
Axes of the slice: x: 4, y: 8, z: 12, core: 2. Of those that a mesh axis runs over, the one named last changes fastest.
Arguments:
- old_field: float32 [64, 196608], P(None, ('seg', 'sub')), may hold values from -1.5 to 1.5
- adapt_flag: int32 [196608], P(('seg', 'sub')), may hold values from 0 to 2, as said below
- family_level: int32 [24576], P(('seg', 'sub')), may hold values from 6 to 8
- face_list: int32 [6, 282624], P(None, ('seg', 'sub')), may hold values from 0 to 1391, as said below
- face_code: int32 [6, 282624], P(None, ('seg', 'sub')), may hold values from 0 to 9, as said below
- send_list: int32 [8, 98304], P(None, ('seg', 'sub')), may hold values from 0 to 367
Outputs:
- new_field: float32 [64, 282624], P(None, ('seg', 'sub'))
- applied: float32 [64, 282624], P(None, ('seg', 'sub'))
The draws below stay inside these ranges and needn't reach their ends.
Inputs may be any that keep to these rules, and one draw needn't show every extreme that they name: `adapt_flag`: 0 keeps a cell, 1 refines it, 2 coarsens it; flag 2 stands on all 8 cells of an aligned family or on none. The cells of all devices before device d (over seg, then sub) give d * 368 + s_d new cells, where s_d is a multiple of 7 from -28 to 28, s_0 = 0, and both ends are reached on some device; all cells together give 282624 new cells; a device coarsens at most 4 families. `face_list`: an entry below 368 names another local cell of the same device; an entry e of 368 or more names ghost slot e - 368, and each of a device's 1024 ghost slots is named by exactly one face of one of its cells. Entries of faces with code 9 are not read. `face_code`: code 9 never stands on a face that names a ghost slot.
All inputs are finite; a program needn't handle non-finite values.
Results may differ from the reference program's by a relative error of at most 0.0003.
Values sent between devices are 32-bit elements; how exact they have to be, the bound alone decides.
No kernel may reach another device: no remote copies, remote signals or barrier semaphores. Data moves between devices by JAX's collectives and lax.ppermute only.
A program may use at most 32 MiB of HBM per device.

```python
import math
import jax
import jax.numpy as jnp
from jax import lax

CELLS_OLD = 256
NET_REFINE = 16
SHIFT_MOST = 28
COARSEN_MOST = 4
CELLS_NEW = 368
GHOST_SLOTS = 128
GHOSTS_ALL = 1024
OLD_TOTAL = 196608
NEW_TOTAL = 282624
SEND_TOTAL = 98304
LEVEL_LOW = 6
LEVEL_HIGH = 8
N_SEG = 96
N_SUB = 8


def face_tables(key):
    device_count = NEW_TOTAL // CELLS_NEW
    pair_count = 6 * CELLS_NEW

    def one_device(sub_key):
        order_key, step_key, code_key, boundary_key = jax.random.split(sub_key, 4)
        pair_order = jax.random.permutation(order_key, pair_count)
        position = jnp.zeros((pair_count,), jnp.int32).at[pair_order].set(jnp.arange(pair_count, dtype=jnp.int32))
        is_ghost = position < GHOSTS_ALL
        pair_cell = jnp.arange(pair_count, dtype=jnp.int32) % CELLS_NEW
        pair_step = jax.random.randint(step_key, (pair_count,), 1, CELLS_NEW)
        local_index = (pair_cell + pair_step) % CELLS_NEW
        neighbour = jnp.where(is_ghost, CELLS_NEW + position, local_index).astype(jnp.int32)
        pair_code = jax.random.randint(code_key, (pair_count,), 0, 9)
        boundary = jax.random.randint(boundary_key, (pair_count,), 0, 10) == 0
        pair_code = jnp.where(is_ghost | jnp.logical_not(boundary), pair_code, 9).astype(jnp.int32)
        return (neighbour.reshape(6, CELLS_NEW), pair_code.reshape(6, CELLS_NEW))
    device_keys = jax.random.split(key, device_count)
    neighbours, pair_codes = jax.vmap(one_device)(device_keys)
    return (jnp.transpose(neighbours, (1, 0, 2)).reshape(6, NEW_TOTAL), jnp.transpose(pair_codes, (1, 0, 2)).reshape(6, NEW_TOTAL))


def draw_face_list(key, part):
    neighbours, pair_codes = face_tables(key)
    return neighbours


def draw_face_code(key, part):
    neighbours, pair_codes = face_tables(key)
    return pair_codes


def draw_adapt_flag(key, part):
    key = jax.random.fold_in(key, 11)
    device_count = OLD_TOTAL // CELLS_OLD
    families = CELLS_OLD // 8
    step_most = SHIFT_MOST // 7
    shift_key, pick_key, count_key, refine_key = jax.random.split(key, 4)
    shift_steps = jax.random.randint(shift_key, (device_count + 1,), -step_most, step_most + 1)
    chosen = jax.random.randint(pick_key, (2,), 0, device_count - 1)
    high_place = 1 + chosen[0]
    low_place = 1 + (chosen[0] + 1 + chosen[1] % (device_count - 2)) % (device_count - 1)
    places = jnp.arange(device_count + 1)
    shift_steps = jnp.where(places == high_place, step_most, shift_steps)
    shift_steps = jnp.where(places == low_place, -step_most, shift_steps)
    shift_steps = jnp.where((places == 0) | (places == device_count), 0, shift_steps)
    target = NET_REFINE + shift_steps[1:] - shift_steps[:-1]
    merges = jax.random.randint(count_key, (device_count,), 0, COARSEN_MOST + 1)
    refines = target + merges

    def one_device(sub_key, merge_count, refine_count):
        family_key, cell_key = jax.random.split(sub_key)
        family_rank = jax.random.permutation(family_key, families)
        merged_cells = jnp.repeat(family_rank < merge_count, 8)
        cell_order = jax.random.permutation(cell_key, CELLS_OLD)
        cell_score = cell_order + jnp.where(merged_cells, CELLS_OLD, 0)
        cell_rank = jnp.argsort(jnp.argsort(cell_score))
        refined = cell_rank < refine_count
        return jnp.where(merged_cells, 2, jnp.where(refined, 1, 0)).astype(jnp.int32)
    device_keys = jax.random.split(refine_key, device_count)
    all_flags = jax.vmap(one_device)(device_keys, merges, refines)
    return all_flags.reshape(OLD_TOTAL)


def set_ends(values, stream_key, smallest, top_value):
    index_at = [jax.random.randint(jax.random.fold_in(stream_key, axis), (), 0, length) for axis, length in enumerate(values.shape)]
    widest = values.shape.index(max(values.shape))
    next_to = index_at[:widest] + [(index_at[widest] + 1) % values.shape[widest]] + index_at[widest + 1:]
    return values.at[tuple(index_at)].set(smallest).at[tuple(next_to)].set(top_value)


def block_levels(stream_key, extent, cuts, low, largest):
    loudness = 1.0
    for dim, blocks in cuts:
        steps = jax.random.uniform(jax.random.fold_in(jax.random.fold_in(stream_key, 6), dim), (blocks,), jnp.float32, low / len(cuts), largest / len(cuts))
        loudness = loudness * jnp.repeat(jnp.exp(steps), extent[dim] // blocks).reshape((-1,) + (1,) * (len(extent) - 1 - dim))
    return loudness


def centred(own_key, dims, width, most, shards=(), held_as=jnp.bfloat16):
    values = width * jax.random.normal(own_key, dims, jnp.float32)
    if shards:
        values = values * block_levels(own_key, dims, shards, -0.22, 0.18)
    return jnp.clip(values, -most, most).astype(held_as)


def setup_inputs(seed: int = 0) -> dict:
    key_of = jax.random.split(jax.random.key(seed), 7)
    return {
        "old_field": centred(key_of[0], (64, OLD_TOTAL), 0.25, 1.5, ((1, 768),), jnp.float32),
        "adapt_flag": draw_adapt_flag(jax.random.fold_in(key_of[6], 71), 0),
        "family_level": set_ends(jax.random.randint(key_of[2], (OLD_TOTAL // 8,), LEVEL_LOW, LEVEL_HIGH + 1), jax.random.fold_in(key_of[2], 1), LEVEL_LOW, LEVEL_HIGH).astype(jnp.int32),
        "face_list": draw_face_list(jax.random.fold_in(key_of[6], 71), 0),
        "face_code": draw_face_code(jax.random.fold_in(key_of[6], 71), 0),
        "send_list": set_ends(jax.random.randint(key_of[5], (N_SUB, SEND_TOTAL), 0, CELLS_NEW), jax.random.fold_in(key_of[5], 1), 0, CELLS_NEW - 1).astype(jnp.int32),
    }


PENALTY = 4.0
TRACE_FORMS = ('i,ijkn->jkn', 'j,ijkn->ikn', 'k,ijkn->ijn')
LIFT_FORMS = ('i,jkn->ijkn', 'j,ikn->ijkn', 'k,ijn->ijkn')
GAUSS_HALF = ((0.1834346424956498, 0.362683783378362), (0.525532409916329, 0.3137066458778873), (0.7966664774136267, 0.2223810344533745), (0.9602898564975363, 0.1012285362903763))

def basis_value(degree, point):
    forms = (1.0, point, 0.5 * (3.0 * point * point - 1.0), 0.5 * (5.0 * point ** 3 - 3.0 * point))
    return forms[degree] * math.sqrt(degree + 0.5)

def basis_slope(degree, point):
    forms = (0.0, 1.0, 3.0 * point, 0.5 * (15.0 * point * point - 3.0))
    return forms[degree] * math.sqrt(degree + 0.5)

def legendre_tables():
    nodes = []
    for point, weight in GAUSS_HALF:
        nodes.append((point, weight))
        nodes.append((-point, weight))
    prolong_table = [[[sum((weight * basis_value(first, point) * basis_value(second, (point + 2.0 * half_index - 1.0) / 2.0) for point, weight in nodes)) for second in range(4)] for first in range(4)] for half_index in range(2)]
    stiff_table = [[sum((weight * basis_slope(first, point) * basis_slope(second, point) for point, weight in nodes)) for second in range(4)] for first in range(4)]
    edge_table = [[basis_value(degree, 2.0 * side - 1.0) for degree in range(4)] for side in range(2)]
    return (jnp.asarray(prolong_table, dtype=jnp.float32), jnp.asarray(stiff_table, dtype=jnp.float32), jnp.asarray(edge_table, dtype=jnp.float32))

def restrict_families(raw_cells, prolong_table):
    families = raw_cells.shape[1] // 8
    children = raw_cells.reshape(4, 4, 4, families, 2, 2, 2)
    partial_value = jnp.einsum('xia,ijkfxyz->ajkfyz', prolong_table, children, precision=lax.Precision.HIGHEST)
    partial_value = jnp.einsum('yjb,ajkfyz->abkfz', prolong_table, partial_value, precision=lax.Precision.HIGHEST)
    partial_value = jnp.einsum('zkc,abkfz->abcf', prolong_table, partial_value, precision=lax.Precision.HIGHEST)
    return (0.125 * partial_value).reshape(64, families)

def compact_records(raw_cells, raw_flag, raw_level, prolong_table):
    total = raw_cells.shape[1]
    families = total // 8
    parents = restrict_families(raw_cells, prolong_table)
    merged = raw_flag.reshape(families, 8)[:, 0] == 2
    family_count = jnp.where(merged, 1, 8).astype(jnp.int32)
    family_end = jnp.cumsum(family_count).astype(jnp.int32)
    slot_ids = jnp.arange(total, dtype=jnp.int32)
    family = jnp.searchsorted(family_end, slot_ids, side='right').astype(jnp.int32)
    live_slot = family < families
    family = jnp.minimum(family, families - 1)
    within = slot_ids - (family_end[family] - family_count[family])
    source = jnp.clip(family * 8 + within, 0, total - 1)
    family_merged = merged[family]
    values = jnp.where(family_merged[None, :], parents[:, family], raw_cells[:, source])
    values = jnp.where(live_slot[None, :], values, 0.0)
    refine = live_slot & jnp.logical_not(family_merged) & (raw_flag[source] == 1)
    rec_level = raw_level[source] + refine.astype(jnp.int32) - family_merged.astype(jnp.int32)
    counts = jnp.where(live_slot, jnp.where(refine, 8, 1), 0).astype(jnp.int32)
    return (values, counts, rec_level)

def prolong_cells(parents, bit_x, bit_y, bit_z, prolong_table):
    halves = jnp.einsum('hia,ajkn->hijkn', prolong_table, parents, precision=lax.Precision.HIGHEST)
    partial_value = jnp.where(bit_x == 1, halves[1], halves[0])
    halves = jnp.einsum('hjb,ibkn->hijkn', prolong_table, partial_value, precision=lax.Precision.HIGHEST)
    partial_value = jnp.where(bit_y == 1, halves[1], halves[0])
    halves = jnp.einsum('hkc,ijcn->hijkn', prolong_table, partial_value, precision=lax.Precision.HIGHEST)
    return jnp.where(bit_z == 1, halves[1], halves[0])

def expand_cells(values, counts, rec_level, record_ends, targets, prolong_table):
    record = jnp.searchsorted(record_ends, targets, side='right').astype(jnp.int32)
    record = jnp.minimum(record, counts.shape[0] - 1)
    within = targets - (record_ends[record] - counts[record])
    parents = values[:, record].reshape(4, 4, 4, -1)
    children = prolong_cells(parents, within // 4, within // 2 % 2, within % 2, prolong_table)
    new_cells = jnp.where(counts[record] == 8, children, parents)
    return (new_cells.reshape(64, -1), rec_level[record])

def map_trace(trace, face_codes, prolong_table):
    offset = jnp.clip(jnp.where(face_codes >= 5, face_codes - 5, face_codes - 1), 0, 3)
    first_bit = offset // 2
    second_bit = offset % 2
    halves = jnp.einsum('hpr,rqn->hpqn', prolong_table, trace, precision=lax.Precision.HIGHEST)
    upper_half = jnp.where(first_bit == 1, halves[1], halves[0])
    halves = jnp.einsum('hqs,psn->hpqn', prolong_table, upper_half, precision=lax.Precision.HIGHEST)
    coarse = jnp.where(second_bit == 1, halves[1], halves[0])
    halves = jnp.einsum('hrp,rqn->hpqn', prolong_table, trace, precision=lax.Precision.HIGHEST)
    lower_half = jnp.where(first_bit == 1, halves[1], halves[0])
    halves = jnp.einsum('hsq,psn->hpqn', prolong_table, lower_half, precision=lax.Precision.HIGHEST)
    finer = 0.25 * jnp.where(second_bit == 1, halves[1], halves[0])
    return jnp.where(face_codes == 0, trace, jnp.where(face_codes <= 4, coarse, jnp.where(face_codes <= 8, finer, 0.0)))

def level_scale(levels):
    size_scale = jnp.zeros(levels.shape, jnp.float32)
    for level_value in range(LEVEL_LOW - 1, LEVEL_HIGH + 2):
        size_scale = jnp.where(levels == level_value, 2.0 ** (LEVEL_LOW + 1 - level_value), size_scale)
    return size_scale

def apply_cells(new_cells, levels, neighbour_of, face_codes, tables):
    prolong_table, stiff_table, edge_table = tables
    modes_grid = new_cells.reshape(4, 4, 4, -1)
    result = jnp.einsum('ai,ijkn->ajkn', stiff_table, modes_grid, precision=lax.Precision.HIGHEST)
    result = result + jnp.einsum('bj,ijkn->ibkn', stiff_table, modes_grid, precision=lax.Precision.HIGHEST)
    result = result + jnp.einsum('ck,ijkn->ijcn', stiff_table, modes_grid, precision=lax.Precision.HIGHEST)
    for face_index in range(6):
        face_axis = face_index // 2
        face_side = face_index % 2
        own_trace = jnp.einsum(TRACE_FORMS[face_axis], edge_table[face_side], modes_grid, precision=lax.Precision.HIGHEST)
        neighbours = neighbour_of(face_index).reshape(4, 4, 4, -1)
        far_trace = jnp.einsum(TRACE_FORMS[face_axis], edge_table[1 - face_side], neighbours, precision=lax.Precision.HIGHEST)
        target = map_trace(far_trace, face_codes[face_index], prolong_table)
        result = result + PENALTY * jnp.einsum(LIFT_FORMS[face_axis], edge_table[face_side], own_trace - target, precision=lax.Precision.HIGHEST)
    return (result * level_scale(levels)).reshape(64, -1)

def reference(old_field, adapt_flag, family_level, face_list, face_code, send_list):
    tables = legendre_tables()
    prolong_table = tables[0]
    cell_level = jnp.repeat(family_level, 8)
    values, counts, rec_level = compact_records(old_field, adapt_flag, cell_level, prolong_table)
    record_ends = jnp.cumsum(counts).astype(jnp.int32)
    device_count = N_SEG * N_SUB
    block_ids = jnp.arange(device_count, dtype=jnp.int32)

    def build_block(block):
        targets = block * CELLS_NEW + jnp.arange(CELLS_NEW, dtype=jnp.int32)
        return expand_cells(values, counts, rec_level, record_ends, targets, prolong_table)
    new_blocks, level_blocks = lax.map(build_block, block_ids)
    new_field = jnp.moveaxis(new_blocks, 0, 1).reshape(64, NEW_TOTAL)
    new_levels = level_blocks.reshape(NEW_TOTAL)
    cell_ids = jnp.arange(NEW_TOTAL, dtype=jnp.int32)
    device_ids = cell_ids // CELLS_NEW
    ghost_index = jnp.maximum(face_list - CELLS_NEW, 0)
    peer_sub = ghost_index // GHOST_SLOTS
    slot_ids = ghost_index % GHOST_SLOTS
    sender = device_ids // N_SUB * N_SUB + peer_sub
    sent_cell = send_list[device_ids % N_SUB, sender * GHOST_SLOTS + slot_ids]
    global_index = jnp.where(face_list < CELLS_NEW, device_ids * CELLS_NEW + face_list, sender * CELLS_NEW + sent_cell).astype(jnp.int32)

    def apply_block(block):
        block_begin = block * CELLS_NEW
        own_cells = lax.dynamic_slice_in_dim(new_field, block_begin, CELLS_NEW, 1)
        own_levels = lax.dynamic_slice_in_dim(new_levels, block_begin, CELLS_NEW, 0)
        link_block = lax.dynamic_slice_in_dim(global_index, block_begin, CELLS_NEW, 1)
        code_block = lax.dynamic_slice_in_dim(face_code, block_begin, CELLS_NEW, 1)

        def neighbour_of(face_index):
            return new_field[:, link_block[face_index]]
        return apply_cells(own_cells, own_levels, neighbour_of, code_block, tables)
    applied = jnp.moveaxis(lax.map(apply_block, block_ids), 0, 1).reshape(64, NEW_TOTAL)
    return (new_field, applied)
```

```python
import functools
import math

import jax
import jax.numpy as jnp
import numpy as np
from jax import lax
from jax.experimental import pallas as pl
from jax.experimental.pallas import tpu as pltpu
from jax.sharding import Mesh
from jax.sharding import PartitionSpec as P

BF = jnp.bfloat16
F32 = jnp.float32
OLD = 256
NEW = 368
PAD = 384
WIDE = 512
SLOTS = 128
SUBS = 8
MOST = 28
LOW = 6
HIGH = 8
PENALTY = 4.0
GAUSS_HALF = (
    (0.1834346424956498, 0.362683783378362),
    (0.525532409916329, 0.3137066458778873),
    (0.7966664774136267, 0.2223810344533745),
    (0.9602898564975363, 0.1012285362903763),
)


def basis_value(degree, point):
    forms = (1.0, point, 0.5 * (3.0 * point * point - 1.0), 0.5 * (5.0 * point**3 - 3.0 * point))
    return forms[degree] * math.sqrt(degree + 0.5)


def basis_slope(degree, point):
    forms = (0.0, 1.0, 3.0 * point, 0.5 * (15.0 * point * point - 3.0))
    return forms[degree] * math.sqrt(degree + 0.5)


def legendre_tables():
    nodes = [(sign * point, weight) for point, weight in GAUSS_HALF for sign in (1.0, -1.0)]
    prolong = np.zeros((2, 4, 4))
    stiff = np.zeros((4, 4))
    edge = np.zeros((2, 4))
    for i in range(4):
        for j in range(4):
            for half in range(2):
                prolong[half, i, j] = sum(
                    w * basis_value(i, p) * basis_value(j, (p + 2.0 * half - 1.0) / 2.0)
                    for p, w in nodes
                )
            stiff[i, j] = sum(w * basis_slope(i, p) * basis_slope(j, p) for p, w in nodes)
        for side in range(2):
            edge[side, i] = basis_value(i, 2.0 * side - 1.0)
    return prolong, stiff, edge


def halves_of(weights):
    high = np.asarray(weights, np.float32).astype(jnp.bfloat16)
    low = (np.asarray(weights, np.float32) - high.astype(np.float32)).astype(jnp.bfloat16)
    return high, low


def triple(weights):
    high, low = halves_of(weights)
    return np.concatenate([high, low, high], axis=1)


def double(weights):
    high, low = halves_of(weights)
    return np.concatenate([high, low], axis=0)


def build_tables():
    prolong, stiff, edge = legendre_tables()
    eye = np.eye(4)
    children = [(k // 4, k // 2 % 2, k % 2) for k in range(8)]
    refine = np.concatenate(
        [np.kron(np.kron(prolong[x], prolong[y]), prolong[z]) for x, y, z in children]
    )
    coarsen = np.concatenate(
        [
            0.125 * np.kron(np.kron(prolong[x].T, prolong[y].T), prolong[z].T)
            for x, y, z in children
        ]
    )

    def along(axis, matrix):
        parts = [eye, eye, eye]
        parts[axis] = matrix
        return np.kron(np.kron(parts[0], parts[1]), parts[2])

    volume = sum(along(axis, stiff) for axis in range(3))
    traces = []
    lifts = []
    for face in range(6):
        axis, side = face // 2, face % 2
        volume = volume + PENALTY * along(axis, np.outer(edge[side], edge[side]))
        traces.append(along(axis, edge[1 - side][None, :]))
        lift = along(axis, edge[side][:, None])
        maps = [np.eye(16)]
        for o in range(4):
            maps.append(np.kron(prolong[o // 2], prolong[o % 2]))
        for o in range(4):
            maps.append(0.25 * np.kron(prolong[o // 2].T, prolong[o % 2].T))
        lifts.extend(-PENALTY * lift @ m for m in maps)
    return (
        triple(coarsen),
        triple(refine),
        triple(np.concatenate(traces)),
        triple(volume),
        double(np.concatenate(lifts, axis=1)),
    )


COARSEN, REFINE, TRACES, VOLUME, LIFTS = build_tables()


def dot(a, b):
    return jnp.dot(a, b, preferred_element_type=F32)


def dot_rows(a, b):
    return lax.dot_general(a, b, (((1,), (1,)), ((), ())), preferred_element_type=F32)


def split(x):
    high = x.astype(BF)
    return high, (x - high.astype(F32)).astype(BF)


def apply_triple(weights, x):
    high, low = split(x)
    return dot(weights, jnp.concatenate([high, high, low], axis=0))


def iota(shape, axis):
    return lax.broadcasted_iota(jnp.int32, shape, axis)


def one_hot(mask):
    return jnp.where(mask, 1.0, 0.0).astype(BF)


def expand_kernel(x_ref, flag_ref, level_ref, coarsen_ref, refine_ref, cells_ref, head_ref, tail_ref):
    x = x_ref[...]
    flag = flag_ref[...]
    lane = iota((1, OLD), 1)
    child = lane % 8
    merged = flag == 2
    first = child == 0
    count = jnp.where(flag == 1, 8.0, jnp.where(merged, jnp.where(first, 1.0, 0.0), 1.0))
    back = jnp.where(merged & ~first, 1.0, 0.0)
    width = jnp.where(flag == 1, 8.0, 1.0)
    level8 = jnp.broadcast_to(level_ref[...].astype(F32), (8, OLD // 8)).astype(BF)
    level = dot(level8, one_hot(iota((OLD // 8, OLD), 0) == iota((OLD // 8, OLD), 1) // 8))[0:1]

    rows8 = jnp.concatenate(
        [count, back, width, jnp.zeros((13, OLD), F32)], axis=0
    ).astype(BF)
    row_id, col_id = iota((OLD, OLD), 0), iota((OLD, OLD), 1)
    sums_col = dot_rows(one_hot(col_id < row_id), rows8)
    same_col = dot_rows(one_hot(col_id == row_id), rows8)
    sums_row = dot(rows8, one_hot(row_id < col_id))[0:1]
    start_col = sums_col[:, 0:1] - same_col[:, 1:2]
    end_col = start_col + same_col[:, 2:3]
    target = iota((1, WIDE), 1).astype(F32)
    chosen = one_hot((target >= start_col) & (target < end_col))

    parts = apply_triple(coarsen_ref[...], x)
    restricted = jnp.where(first, parts[0:64], 0.0)
    for k in range(1, 8):
        restricted = restricted + jnp.where(child == k, parts[64 * k : 64 * k + 64], 0.0)
    source = jnp.where(merged, restricted, x)
    high, low = split(source)
    refined = jnp.where(flag == 1, 1.0, 0.0)
    new_level = level + refined - jnp.where(merged, 1.0, 0.0)
    coarse_start = jnp.floor(sums_row * 0.0625)
    fine_start = sums_row - 16.0 * coarse_start
    info = jnp.concatenate([coarse_start, fine_start, new_level, refined], axis=0)
    info = jnp.where(merged & ~first, 0.0, info)
    info = jnp.concatenate([info, jnp.zeros((12, OLD), F32)], axis=0).astype(BF)
    picked = dot(jnp.concatenate([high, low, info], axis=0), chosen)
    record = picked[0:64] + picked[64:128]
    place = target - 16.0 * picked[128:129] - picked[129:130]
    is_refined = picked[131:132] > 0.5
    outs = apply_triple(refine_ref[...], record)
    fine = jnp.where(place == 0.0, outs[0:64], 0.0)
    for k in range(1, 8):
        fine = fine + jnp.where(place == float(k), outs[64 * k : 64 * k + 64], 0.0)
    cells = jnp.where(is_refined, fine, record)
    cells = jnp.concatenate([cells, jnp.broadcast_to(picked[130:131], (8, WIDE))], axis=0)
    cells_ref[...] = cells
    head_ref[...] = cells[:, 0:128]
    total = jnp.sum(count).astype(jnp.int32)
    tail_ref[...] = pltpu.roll(cells, (MOST - total) & (WIDE - 1), 1)[:, 0:128]


def place_kernel(
    ids_ref, near_ref, far_ref, cells_ref, before_ref, after_ref, send_ref, new_ref, pad_ref, out_ref
):
    near = near_ref[...]
    place = iota(near.shape, 0)
    inner = ids_ref[0]
    earlier = jnp.sum(jnp.where(place < inner, near, 0.0), axis=0, keepdims=True)
    own = jnp.sum(jnp.where(place == inner, near, 0.0), axis=0, keepdims=True)
    far = far_ref[...]
    earlier = earlier + jnp.sum(
        jnp.where(iota(far.shape, 0) < ids_ref[1], far, 0.0), axis=0, keepdims=True
    )
    shift = jnp.max(earlier).astype(jnp.int32) - ids_ref[2]
    end = shift + jnp.max(own).astype(jnp.int32)
    rolled = pltpu.roll(cells_ref[...], shift & (WIDE - 1), 1)
    before = pltpu.roll(before_ref[...], (shift - MOST) & 127, 1)
    after = pltpu.roll(after_ref[...], end & 127, 1)
    lane = iota((1, 128), 1)
    cells = jnp.concatenate(
        [
            jnp.where(lane < shift, before, rolled[:, 0:128]),
            rolled[:, 128:256],
            jnp.where(lane + 256 >= end, after, rolled[:, 256:384]),
        ],
        axis=1,
    )
    new_ref[...] = cells[0:64, 0:NEW]
    pad_ref[...] = cells
    high, low = split(cells[0:64])
    both = jnp.concatenate([high, low], axis=0)
    source = iota((PAD, SLOTS), 0)
    for peer in range(SUBS):
        sent = dot(both, one_hot(source == send_ref[peer : peer + 1, :]))
        out_ref[peer] = sent[0:64] + sent[64:128]


def apply_kernel(pad_ref, ghost_ref, face_ref, code_ref, traces_ref, volume_ref, lifts_ref, out_ref):
    cells = pad_ref[0:64, :]
    ghosts = [ghost_ref[peer] for peer in range(SUBS)]
    traces = apply_triple(traces_ref[...], jnp.concatenate([cells] + ghosts, axis=1))
    high, low = split(traces)
    total = PAD + SUBS * SLOTS
    source = iota((total, NEW), 0)
    face_list = face_ref[...]
    face_list = jnp.where(face_list >= NEW, face_list + (PAD - NEW), face_list)
    codes = code_ref[...]
    highs, lows = [], []
    for face in range(6):
        rows = slice(16 * face, 16 * face + 16)
        both = jnp.concatenate([high[rows], low[rows]], axis=0)
        far = dot(both, one_hot(source == face_list[face : face + 1]))
        code = codes[face : face + 1]
        for value in range(9):
            kept = jnp.where(code == value, far, 0.0).astype(BF)
            highs.append(kept[0:16])
            lows.append(kept[16:32])
    lifts = lifts_ref[...]
    upper = dot(lifts, jnp.concatenate(highs, axis=0))
    lower = dot(lifts[0:64], jnp.concatenate(lows, axis=0))
    body = apply_triple(volume_ref[...], cells[:, 0:NEW])
    result = body + upper[0:64] + upper[64:128] + lower
    level = pad_ref[64:65, 0:NEW]
    scale = jnp.zeros((1, NEW), F32)
    for value in range(LOW - 1, HIGH + 2):
        scale = jnp.where(level == float(value), 2.0 ** (LOW + 1 - value), scale)
    out_ref[...] = result * scale


def whole():
    return pl.BlockSpec(memory_space=pltpu.VMEM)


def shape(*dims):
    return jax.ShapeDtypeStruct(dims, F32)


PARAMS = pltpu.CompilerParams(vmem_limit_bytes=48 * 1024 * 1024)


def on_device(old_field, adapt_flag, family_level, face_list, face_code, send_list):
    inner = lax.axis_index(("xc", "sub"))
    outer = lax.axis_index("z")
    inner_size = lax.axis_size("xc") * lax.axis_size("sub")
    outer_size = lax.axis_size("z")
    ids = jnp.stack([inner, outer, (outer * inner_size + inner) * NEW]).astype(jnp.int32)

    first = jnp.arange(OLD, dtype=jnp.int32) % 8 == 0
    counts = jnp.where(adapt_flag == 1, 8, jnp.where((adapt_flag == 2) & ~first, 0, 1))
    produced = jnp.sum(counts).astype(F32)
    with jax.named_scope("counts_inner"):
        near = lax.all_to_all(
            jnp.broadcast_to(produced, (inner_size, 128)), ("xc", "sub"), 0, 0, tiled=True
        )
    with jax.named_scope("counts_outer"):
        sums = jnp.sum(near, axis=0, keepdims=True)
        far = lax.all_to_all(jnp.broadcast_to(sums, (outer_size, 128)), "z", 0, 0, tiled=True)

    cells, head, tail = pl.pallas_call(
        expand_kernel,
        out_shape=(shape(72, WIDE), shape(72, 128), shape(72, 128)),
        in_specs=[whole()] * 5,
        out_specs=(whole(), whole(), whole()),
        compiler_params=PARAMS,
        name="expand",
    )(
        old_field,
        adapt_flag.reshape(1, OLD),
        family_level.reshape(1, OLD // 8),
        jnp.asarray(COARSEN),
        jnp.asarray(REFINE),
    )
    everything = ("z", "xc", "sub")
    size = outer_size * inner_size
    with jax.named_scope("curve_halo"):
        before = lax.ppermute(tail, everything, [(i, i + 1) for i in range(size - 1)])
        after = lax.ppermute(head, everything, [(i + 1, i) for i in range(size - 1)])

    new_field, padded, outgoing = pl.pallas_call(
        place_kernel,
        out_shape=(shape(64, NEW), shape(72, PAD), shape(SUBS, 64, SLOTS)),
        in_specs=[pl.BlockSpec(memory_space=pltpu.SMEM)] + [whole()] * 6,
        out_specs=(whole(), whole(), whole()),
        compiler_params=PARAMS,
        name="place",
    )(ids, near, far, cells, before, after, send_list)
    with jax.named_scope("ghosts"):
        ghosts = lax.all_to_all(outgoing, "sub", 0, 0, tiled=True)
    applied = pl.pallas_call(
        apply_kernel,
        out_shape=shape(64, NEW),
        in_specs=[whole()] * 7,
        out_specs=whole(),
        compiler_params=PARAMS,
        name="apply",
    )(
        padded,
        ghosts,
        face_list,
        face_code,
        jnp.asarray(TRACES),
        jnp.asarray(VOLUME),
        jnp.asarray(LIFTS),
    )
    return (new_field, applied)


def solution(mesh):
    seg, sub = mesh.shape["seg"], mesh.shape["sub"]
    inner = 8
    finer = Mesh(mesh.devices.reshape(seg // inner, inner, sub), ("z", "xc", "sub"))
    flat = ("z", "xc", "sub")
    row, cols = P(flat), P(None, flat)
    return jax.shard_map(
        on_device,
        mesh=finer,
        in_specs=(cols, row, row, cols, cols, cols),
        out_specs=(cols, cols),
        check_vma=False,
    )
```

```python
import math

import jax
import jax.numpy as jnp
import numpy as np
from jax import lax
from jax.experimental import pallas as pl
from jax.experimental.pallas import tpu as pltpu
from jax.sharding import Mesh
from jax.sharding import PartitionSpec as P

BF = jnp.bfloat16
F32 = jnp.float32
OLD = 256
NEW = 368
PAD = 384
WIDE = 512
SLOTS = 128
SUBS = 8
GROUP = 64
MOST = 28
LOW = 6
HIGH = 8
PENALTY = 4.0
GAUSS_HALF = (
    (0.1834346424956498, 0.362683783378362),
    (0.525532409916329, 0.3137066458778873),
    (0.7966664774136267, 0.2223810344533745),
    (0.9602898564975363, 0.1012285362903763),
)


def basis_value(degree, point):
    forms = (1.0, point, 0.5 * (3.0 * point * point - 1.0), 0.5 * (5.0 * point**3 - 3.0 * point))
    return forms[degree] * math.sqrt(degree + 0.5)


def basis_slope(degree, point):
    forms = (0.0, 1.0, 3.0 * point, 0.5 * (15.0 * point * point - 3.0))
    return forms[degree] * math.sqrt(degree + 0.5)


def legendre_tables():
    nodes = [(sign * point, weight) for point, weight in GAUSS_HALF for sign in (1.0, -1.0)]
    prolong = np.zeros((2, 4, 4))
    stiff = np.zeros((4, 4))
    edge = np.zeros((2, 4))
    for i in range(4):
        for j in range(4):
            for half in range(2):
                prolong[half, i, j] = sum(
                    w * basis_value(i, p) * basis_value(j, (p + 2.0 * half - 1.0) / 2.0)
                    for p, w in nodes
                )
            stiff[i, j] = sum(w * basis_slope(i, p) * basis_slope(j, p) for p, w in nodes)
        for side in range(2):
            edge[side, i] = basis_value(i, 2.0 * side - 1.0)
    return prolong, stiff, edge


def halves_of(weights):
    high = np.asarray(weights, np.float32).astype(jnp.bfloat16)
    low = (np.asarray(weights, np.float32) - high.astype(np.float32)).astype(jnp.bfloat16)
    return high, low


def triple(weights):
    high, low = halves_of(weights)
    return np.concatenate([high, low, high], axis=1)


def double(weights):
    high, low = halves_of(weights)
    return np.concatenate([high, low], axis=0)


def build_tables():
    prolong, stiff, edge = legendre_tables()
    eye = np.eye(4)
    children = [(k // 4, k // 2 % 2, k % 2) for k in range(8)]
    refine = np.concatenate(
        [np.kron(np.kron(prolong[x], prolong[y]), prolong[z]) for x, y, z in children]
    )
    coarsen = np.concatenate(
        [
            0.125 * np.kron(np.kron(prolong[x].T, prolong[y].T), prolong[z].T)
            for x, y, z in children
        ]
    )

    def along(axis, matrix):
        parts = [eye, eye, eye]
        parts[axis] = matrix
        return np.kron(np.kron(parts[0], parts[1]), parts[2])

    maps = [np.eye(16)]
    maps.extend(np.kron(prolong[o // 2], prolong[o % 2]) for o in range(4))
    maps.extend(0.25 * np.kron(prolong[o // 2].T, prolong[o % 2].T) for o in range(4))
    volume = sum(along(axis, stiff) for axis in range(3))
    traces = []
    lifts = []
    for face in range(6):
        axis, side = face // 2, face % 2
        volume = volume + PENALTY * along(axis, np.outer(edge[side], edge[side]))
        traces.append(along(axis, edge[1 - side][None, :]))
        lifts.append(-PENALTY * along(axis, edge[side][:, None]))
    return (
        triple(coarsen),
        triple(refine),
        triple(np.concatenate(traces)),
        triple(np.concatenate(maps)),
        triple(volume),
        double(np.concatenate([lift @ m for lift in lifts for m in maps], axis=1)),
        double(np.concatenate(lifts, axis=1)),
    )


COARSEN, REFINE, TRACES, MAPS, VOLUME, LIFTED_MAPS, LIFTS = build_tables()


def dot(a, b):
    return jnp.dot(a, b, preferred_element_type=F32)


def dot_rows(a, b):
    return lax.dot_general(a, b, (((1,), (1,)), ((), ())), preferred_element_type=F32)


def split(x):
    high = x.astype(BF)
    return high, (x - high.astype(F32)).astype(BF)


def apply_triple(weights, x):
    high, low = split(x)
    return dot(weights, jnp.concatenate([high, high, low], axis=0))


def iota(shape, axis):
    return lax.broadcasted_iota(jnp.int32, shape, axis)


def one_hot(mask):
    return jnp.where(mask, 1.0, 0.0).astype(BF)


def expand(x_ref, flag_ref, level_ref, coarsen_ref, refine_ref, cells_ref, head_ref, tail_ref):
    x = x_ref[...]
    flag = flag_ref[...]
    lane = iota((1, OLD), 1)
    child = lane % 8
    merged = flag == 2
    first = child == 0
    count = jnp.where(flag == 1, 8.0, jnp.where(merged, jnp.where(first, 1.0, 0.0), 1.0))
    back = jnp.where(merged & ~first, 1.0, 0.0)
    width = jnp.where(flag == 1, 8.0, 1.0)
    level8 = jnp.broadcast_to(level_ref[...].astype(F32), (8, OLD // 8)).astype(BF)
    level = dot(level8, one_hot(iota((OLD // 8, OLD), 0) == iota((OLD // 8, OLD), 1) // 8))[0:1]

    rows8 = jnp.concatenate(
        [count, back, width, jnp.zeros((13, OLD), F32)], axis=0
    ).astype(BF)
    row_id, col_id = iota((OLD, OLD), 0), iota((OLD, OLD), 1)
    sums_col = dot_rows(one_hot(col_id < row_id), rows8)
    same_col = dot_rows(one_hot(col_id == row_id), rows8)
    sums_row = dot(rows8, one_hot(row_id < col_id))[0:1]
    start_col = sums_col[:, 0:1] - same_col[:, 1:2]
    end_col = start_col + same_col[:, 2:3]
    target = iota((1, WIDE), 1).astype(F32)
    chosen = one_hot((target >= start_col) & (target < end_col))

    parts = apply_triple(coarsen_ref[...], x)
    restricted = jnp.where(first, parts[0:64], 0.0)
    for k in range(1, 8):
        restricted = restricted + jnp.where(child == k, parts[64 * k : 64 * k + 64], 0.0)
    source = jnp.where(merged, restricted, x)
    high, low = split(source)
    refined = jnp.where(flag == 1, 1.0, 0.0)
    new_level = level + refined - jnp.where(merged, 1.0, 0.0)
    coarse_start = jnp.floor(sums_row * 0.0625)
    fine_start = sums_row - 16.0 * coarse_start
    info = jnp.concatenate([coarse_start, fine_start, new_level, refined], axis=0)
    info = jnp.where(merged & ~first, 0.0, info)
    info = jnp.concatenate([info, jnp.zeros((12, OLD), F32)], axis=0).astype(BF)
    picked = dot(jnp.concatenate([high, low, info], axis=0), chosen)
    record = picked[0:64] + picked[64:128]
    place = target - 16.0 * picked[128:129] - picked[129:130]
    is_refined = picked[131:132] > 0.5
    outs = apply_triple(refine_ref[...], record)
    fine = jnp.where(place == 0.0, outs[0:64], 0.0)
    for k in range(1, 8):
        fine = fine + jnp.where(place == float(k), outs[64 * k : 64 * k + 64], 0.0)
    cells = jnp.where(is_refined, fine, record)
    cells = jnp.concatenate([cells, jnp.broadcast_to(picked[130:131], (8, WIDE))], axis=0)
    cells_ref[...] = cells
    head_ref[...] = cells[:, 0:128]
    total = jnp.sum(count).astype(jnp.int32)
    tail_ref[...] = pltpu.roll(cells, (MOST - total) & (WIDE - 1), 1)[:, 0:128]


def request(flag_ref, face_ref, code_ref, out_ref, slot_ref):
    flag = flag_ref[...]
    first = iota((1, OLD), 1) % 8 == 0
    count = jnp.where(flag == 1, 8.0, jnp.where((flag == 2) & ~first, 0.0, 1.0))
    produced = jnp.broadcast_to(jnp.sum(count, axis=1, keepdims=True), (GROUP, SLOTS))
    codes = code_ref[...]
    ghost = jnp.where(codes == 9, -1, face_ref[...] - NEW)
    cell = iota((1, NEW), 1)
    cell_high = (cell // 16).astype(F32)
    cell_low = (cell % 16).astype(F32)
    peers = iota((SUBS, NEW), 0)
    slots = iota((SLOTS, NEW), 0)
    info = jnp.zeros((4 * SUBS, SLOTS), F32)
    for face in range(6):
        entry = ghost[face : face + 1]
        named = (peers == entry // SLOTS) & (entry >= 0)
        code = codes[face : face + 1].astype(F32)
        rows = [jnp.where(named, value, 0.0) for value in (float(face), code, cell_high, cell_low)]
        info = info + dot_rows(
            jnp.concatenate(rows, axis=0).astype(BF), one_hot(slots == entry % SLOTS)
        )
    slot_ref[0:SUBS] = info[0:SUBS]
    slot_ref[SUBS : 2 * SUBS] = info[2 * SUBS : 3 * SUBS] * 16.0 + info[3 * SUBS : 4 * SUBS]
    out_ref[:, 0, 0:SLOTS] = produced
    for part in range(2):
        wanted = info[part * SUBS : (part + 1) * SUBS]
        wanted = jnp.concatenate([wanted] * (GROUP // SUBS), axis=0)
        out_ref[:, 0, (part + 1) * SLOTS : (part + 2) * SLOTS] = wanted


def start_kernel(*refs):
    sources, refs = refs[0:7], refs[7:]
    asked_ref, slot_ref, cells_ref, head_ref, tail_ref = refs[0:5]
    landed, sems = refs[5:12], refs[12]
    copies = [
        pltpu.make_async_copy(source, target, sems.at[index])
        for index, (source, target) in enumerate(zip(sources, landed))
    ]
    for copy in copies:
        copy.start()
    flag_ref, face_ref, code_ref, level_ref, x_ref, coarsen_ref, refine_ref = landed
    for copy in copies[0:3]:
        copy.wait()
    request(flag_ref, face_ref, code_ref, asked_ref, slot_ref)
    for copy in copies[3:7]:
        copy.wait()
    expand(x_ref, flag_ref, level_ref, coarsen_ref, refine_ref, cells_ref, head_ref, tail_ref)


def total_kernel(near_ref, out_ref):
    total = jnp.sum(near_ref[:, 0:SLOTS], axis=0, keepdims=True)
    for place in range(out_ref.shape[0]):
        out_ref[place] = total


def choose_kernel(send_ref, out_ref):
    source = iota((PAD, SLOTS), 0)
    for peer in range(SUBS):
        out_ref[:, peer * SLOTS : (peer + 1) * SLOTS] = one_hot(source == send_ref[peer : peer + 1, :])


def place_kernel(
    ids_ref,
    near_ref,
    far_ref,
    cells_ref,
    before_ref,
    after_ref,
    chosen_ref,
    traces_ref,
    maps_ref,
    new_ref,
    pad_ref,
    trace_ref,
    out_ref,
):
    near = near_ref[:, 0:SLOTS]
    place = iota(near.shape, 0)
    inner = ids_ref[0]
    earlier = jnp.sum(jnp.where(place < inner, near, 0.0), axis=0, keepdims=True)
    own = jnp.sum(jnp.where(place == inner, near, 0.0), axis=0, keepdims=True)
    far = far_ref[...]
    earlier = earlier + jnp.sum(
        jnp.where(iota(far.shape, 0) < ids_ref[1], far, 0.0), axis=0, keepdims=True
    )
    shift = jnp.max(earlier).astype(jnp.int32) - ids_ref[2]
    end = shift + jnp.max(own).astype(jnp.int32)
    rolled = pltpu.roll(cells_ref[...], shift & (WIDE - 1), 1)
    before = pltpu.roll(before_ref[...], (shift - MOST) & 127, 1)
    after = pltpu.roll(after_ref[...], end & 127, 1)
    lane = iota((1, 128), 1)
    cells = jnp.concatenate(
        [
            jnp.where(lane < shift, before, rolled[:, 0:128]),
            rolled[:, 128:256],
            jnp.where(lane + 256 >= end, after, rolled[:, 256:384]),
        ],
        axis=1,
    )
    new_ref[...] = cells[0:64, 0:NEW]
    pad_ref[...] = cells
    high, low = split(apply_triple(traces_ref[...], cells[0:64]))
    both = jnp.concatenate([high, low], axis=0)
    trace_ref[...] = both
    mine = place // SUBS == ids_ref[3]
    wanted = []
    for part in range(2):
        rows = jnp.where(mine, near_ref[:, (part + 1) * SLOTS : (part + 2) * SLOTS], 0.0)
        total = rows[0:SUBS]
        for other in range(1, GROUP // SUBS):
            total = total + rows[other * SUBS : (other + 1) * SUBS]
        wanted.append(total)
    sent = dot(both, chosen_ref[...])
    parts = []
    for peer in range(SUBS):
        lanes = slice(peer * SLOTS, (peer + 1) * SLOTS)
        face = wanted[0][peer : peer + 1]
        picked = jnp.zeros((32, SLOTS), F32)
        for value in range(6):
            rows = jnp.concatenate(
                [sent[16 * value : 16 * value + 16, lanes], sent[96 + 16 * value : 112 + 16 * value, lanes]],
                axis=0,
            )
            picked = jnp.where(face == float(value), rows, picked)
        parts.append(picked.astype(BF))
    picked = jnp.concatenate(parts, axis=1)
    mapped = dot(maps_ref[...], jnp.concatenate([picked[0:16], picked[0:16], picked[16:32]], axis=0))
    for peer in range(SUBS):
        lanes = slice(peer * SLOTS, (peer + 1) * SLOTS)
        code = wanted[1][peer : peer + 1]
        result = mapped[0:16, lanes]
        for value in range(1, 9):
            result = jnp.where(code == float(value), mapped[16 * value : 16 * value + 16, lanes], result)
        out_ref[peer] = result


def inside_kernel(
    pad_ref, trace_ref, face_ref, code_ref, volume_ref, lifts_ref, slot_ref, out_ref, owned_ref
):
    owner = iota((PAD, SLOTS), 0)
    for peer in range(SUBS):
        cell = slot_ref[SUBS + peer : SUBS + peer + 1].astype(jnp.int32)
        owned_ref[:, peer * SLOTS : (peer + 1) * SLOTS] = one_hot(owner == cell)
    traces = trace_ref[...]
    source = iota((PAD, NEW), 0)
    face_list = face_ref[...]
    face_list = jnp.where(face_list >= NEW, -1, face_list)
    codes = code_ref[...]
    highs, lows = [], []
    for face in range(6):
        both = jnp.concatenate(
            [traces[16 * face : 16 * face + 16], traces[96 + 16 * face : 112 + 16 * face]], axis=0
        )
        far = dot(both, one_hot(source == face_list[face : face + 1]))
        code = codes[face : face + 1]
        for value in range(9):
            kept = jnp.where(code == value, far, 0.0).astype(BF)
            highs.append(kept[0:16])
            lows.append(kept[16:32])
    lifts = lifts_ref[...]
    upper = dot(lifts, jnp.concatenate(highs, axis=0))
    lower = dot(lifts[0:64], jnp.concatenate(lows, axis=0))
    body = apply_triple(volume_ref[...], pad_ref[0:64, 0:NEW])
    out_ref[...] = body + upper[0:64] + upper[64:128] + lower


def outside_kernel(pad_ref, base_ref, ghost_ref, slot_ref, owned_ref, lifts_ref, out_ref):
    highs, lows = [], []
    for peer in range(SUBS):
        high, low = split(ghost_ref[peer])
        both = jnp.concatenate([high.astype(F32), low.astype(F32)], axis=0)
        face = slot_ref[peer : peer + 1]
        kept = [jnp.where(face == float(value), both, 0.0).astype(BF) for value in range(6)]
        highs.append(jnp.concatenate([part[0:16] for part in kept], axis=0))
        lows.append(jnp.concatenate([part[16:32] for part in kept], axis=0))
    lifts = lifts_ref[...]
    upper = dot(lifts, jnp.concatenate(highs, axis=1))
    lower = dot(lifts[0:64], jnp.concatenate(lows, axis=1))
    high, low = split(upper[0:64] + upper[64:128] + lower)
    landed = dot_rows(jnp.concatenate([high, low], axis=0), owned_ref[...])
    result = base_ref[...] + (landed[0:64] + landed[64:128])[:, 0:NEW]
    level = pad_ref[64:65, 0:NEW]
    scale = jnp.zeros((1, NEW), F32)
    for value in range(LOW - 1, HIGH + 2):
        scale = jnp.where(level == float(value), 2.0 ** (LOW + 1 - value), scale)
    out_ref[...] = result * scale


def whole():
    return pl.BlockSpec(memory_space=pltpu.VMEM)


def shape(*dims, dtype=F32):
    return jax.ShapeDtypeStruct(dims, dtype)


PARAMS = pltpu.CompilerParams(vmem_limit_bytes=48 * 1024 * 1024)


def call(kernel, out_shape, *operands, scalars=0):
    specs = [pl.BlockSpec(memory_space=pltpu.SMEM)] * scalars
    specs += [whole()] * (len(operands) - scalars)
    return pl.pallas_call(
        kernel,
        out_shape=out_shape,
        in_specs=specs,
        out_specs=jax.tree.map(lambda _: whole(), out_shape),
        compiler_params=PARAMS,
        name=kernel.__name__,
    )(*operands)


def on_device(old_field, adapt_flag, family_level, face_list, face_code, send_list):
    sub = lax.axis_index("sub")
    column = lax.axis_index("xc")
    outer = lax.axis_index("z")
    inner = column * lax.axis_size("sub") + sub
    outer_size = lax.axis_size("z")
    ids = jnp.stack([inner, outer, (outer * GROUP + inner) * NEW, column]).astype(jnp.int32)
    flag = adapt_flag.reshape(1, OLD)

    operands = (
        flag,
        face_list,
        face_code,
        family_level.reshape(1, OLD // 8),
        old_field,
        jnp.asarray(COARSEN),
        jnp.asarray(REFINE),
    )
    asked, slots, cells, head, tail = pl.pallas_call(
        start_kernel,
        out_shape=(
            shape(GROUP, 1, 3 * SLOTS),
            shape(2 * SUBS, SLOTS),
            shape(72, WIDE),
            shape(72, 128),
            shape(72, 128),
        ),
        in_specs=[pl.BlockSpec(memory_space=pltpu.HBM)] * len(operands),
        out_specs=(whole(),) * 5,
        scratch_shapes=[pltpu.VMEM(x.shape, x.dtype) for x in operands]
        + [pltpu.SemaphoreType.DMA((len(operands),))],
        name="start_kernel",
    )(*operands)
    with jax.named_scope("counts_inner"):
        near = lax.all_to_all(asked, ("xc", "sub"), 0, 0, tiled=True).reshape(GROUP, 3 * SLOTS)
    with jax.named_scope("counts_outer"):
        sums = call(total_kernel, shape(outer_size, 1, SLOTS), near)
    everything = ("z", "xc", "sub")
    size = outer_size * GROUP
    head, sums = lax.optimization_barrier((head, sums))
    with jax.named_scope("curve_halo"):
        before = lax.ppermute(tail, everything, [(i, i + 1) for i in range(size - 1)])
        after = lax.ppermute(head, everything, [(i + 1, i) for i in range(size - 1)])
    with jax.named_scope("counts_outer"):
        far = lax.all_to_all(sums, "z", 0, 0, tiled=True).reshape(outer_size, SLOTS)

    chosen = call(choose_kernel, shape(PAD, SUBS * SLOTS, dtype=BF), send_list)
    new_field, padded, traces, outgoing = call(
        place_kernel,
        (
            shape(64, NEW),
            shape(72, PAD),
            shape(192, PAD, dtype=BF),
            shape(SUBS, 16, SLOTS),
        ),
        ids,
        near,
        far,
        cells,
        before,
        after,
        chosen,
        jnp.asarray(TRACES),
        jnp.asarray(MAPS),
        scalars=1,
    )
    with jax.named_scope("ghosts"):
        ghosts = lax.all_to_all(outgoing, "sub", 0, 0, tiled=True)
    base, owned = call(
        inside_kernel,
        (shape(64, NEW), shape(PAD, SUBS * SLOTS, dtype=BF)),
        padded,
        traces,
        face_list,
        face_code,
        jnp.asarray(VOLUME),
        jnp.asarray(LIFTED_MAPS),
        slots,
    )
    applied = call(
        outside_kernel, shape(64, NEW), padded, base, ghosts, slots, owned, jnp.asarray(LIFTS)
    )
    return (new_field, applied)


def solution(mesh):
    seg, sub = mesh.shape["seg"], mesh.shape["sub"]
    columns = GROUP // sub
    finer = Mesh(mesh.devices.reshape(seg // columns, columns, sub), ("z", "xc", "sub"))
    flat = ("z", "xc", "sub")
    row, cols = P(flat), P(None, flat)
    return jax.shard_map(
        on_device,
        mesh=finer,
        in_specs=(cols, row, row, cols, cols, cols),
        out_specs=(cols, cols),
        check_vma=False,
    )
```

```python
import math

import jax
import jax.numpy as jnp
import numpy as np
from jax import lax
from jax.experimental import pallas as pl
from jax.experimental.pallas import tpu as pltpu
from jax.sharding import Mesh
from jax.sharding import PartitionSpec as P

BF = jnp.bfloat16
F32 = jnp.float32
OLD = 256
NEW = 368
PAD = 384
WIDE = 512
SLOTS = 128
SUBS = 8
GROUP = 64
PIECES = 2
MOST = 28
LOW = 6
HIGH = 8
PENALTY = 4.0
GAUSS_HALF = (
    (0.1834346424956498, 0.362683783378362),
    (0.525532409916329, 0.3137066458778873),
    (0.7966664774136267, 0.2223810344533745),
    (0.9602898564975363, 0.1012285362903763),
)


def basis_value(degree, point):
    forms = (1.0, point, 0.5 * (3.0 * point * point - 1.0), 0.5 * (5.0 * point**3 - 3.0 * point))
    return forms[degree] * math.sqrt(degree + 0.5)


def basis_slope(degree, point):
    forms = (0.0, 1.0, 3.0 * point, 0.5 * (15.0 * point * point - 3.0))
    return forms[degree] * math.sqrt(degree + 0.5)


def legendre_tables():
    nodes = [(sign * point, weight) for point, weight in GAUSS_HALF for sign in (1.0, -1.0)]
    prolong = np.zeros((2, 4, 4))
    stiff = np.zeros((4, 4))
    edge = np.zeros((2, 4))
    for i in range(4):
        for j in range(4):
            for half in range(2):
                prolong[half, i, j] = sum(
                    w * basis_value(i, p) * basis_value(j, (p + 2.0 * half - 1.0) / 2.0)
                    for p, w in nodes
                )
            stiff[i, j] = sum(w * basis_slope(i, p) * basis_slope(j, p) for p, w in nodes)
        for side in range(2):
            edge[side, i] = basis_value(i, 2.0 * side - 1.0)
    return prolong, stiff, edge


def halves_of(weights):
    high = np.asarray(weights, np.float32).astype(jnp.bfloat16)
    low = (np.asarray(weights, np.float32) - high.astype(np.float32)).astype(jnp.bfloat16)
    return high, low


def triple(weights):
    high, low = halves_of(weights)
    return np.concatenate([high, low, high], axis=1)


def beside(weights):
    return np.concatenate(halves_of(weights), axis=1)


def double(weights):
    high, low = halves_of(weights)
    return np.concatenate([high, low], axis=0)


def build_tables():
    prolong, stiff, edge = legendre_tables()
    eye = np.eye(4)
    children = [(k // 4, k // 2 % 2, k % 2) for k in range(8)]
    refine = np.concatenate(
        [np.kron(np.kron(prolong[x], prolong[y]), prolong[z]) for x, y, z in children]
    )
    coarsen = np.concatenate(
        [
            0.125 * np.kron(np.kron(prolong[x].T, prolong[y].T), prolong[z].T)
            for x, y, z in children
        ]
    )

    def along(axis, matrix):
        parts = [eye, eye, eye]
        parts[axis] = matrix
        return np.kron(np.kron(parts[0], parts[1]), parts[2])

    maps = [np.eye(16)]
    maps.extend(np.kron(prolong[o // 2], prolong[o % 2]) for o in range(4))
    maps.extend(0.25 * np.kron(prolong[o // 2].T, prolong[o % 2].T) for o in range(4))
    volume = sum(along(axis, stiff) for axis in range(3))
    traces = []
    lifts = []
    for face in range(6):
        axis, side = face // 2, face % 2
        volume = volume + PENALTY * along(axis, np.outer(edge[side], edge[side]))
        traces.append(along(axis, edge[1 - side][None, :]))
        lifts.append(-PENALTY * along(axis, edge[side][:, None]))
    return (
        beside(coarsen),
        beside(refine),
        triple(np.concatenate(traces)),
        triple(np.concatenate(maps)),
        triple(volume),
        double(np.concatenate([lift @ m for lift in lifts for m in maps], axis=1)),
        double(np.concatenate(lifts, axis=1)),
    )


COARSEN, REFINE, TRACES, MAPS, VOLUME, LIFTED_MAPS, LIFTS = build_tables()


def dot(a, b):
    return jnp.dot(a, b, preferred_element_type=F32)


def dot_rows(a, b):
    return lax.dot_general(a, b, (((1,), (1,)), ((), ())), preferred_element_type=F32)


def split(x):
    high = x.astype(BF)
    return high, (x - high.astype(F32)).astype(BF)


def apply_triple(weights, x):
    high, low = split(x)
    return dot(weights, jnp.concatenate([high, high, low], axis=0))


def apply_beside(weights, x):
    high, low = split(x)
    return dot(weights, jnp.concatenate([high, high], axis=0)) + dot(weights[:, 0:64], low)


def iota(shape, axis):
    return lax.broadcasted_iota(jnp.int32, shape, axis)


def one_hot(mask):
    return jnp.where(mask, 1.0, 0.0).astype(BF)


def expand(x_ref, flag_ref, level_ref, coarsen_ref, refine_ref, cells_ref, pair_ref, other_ref):
    x = x_ref[...]
    flag = flag_ref[...]
    lane = iota((1, OLD), 1)
    child = lane % 8
    merged = flag == 2
    first = child == 0
    count = jnp.where(flag == 1, 8.0, jnp.where(merged, jnp.where(first, 1.0, 0.0), 1.0))
    back = jnp.where(merged & ~first, 1.0, 0.0)
    width = jnp.where(flag == 1, 8.0, 1.0)
    level8 = jnp.broadcast_to(level_ref[...].astype(F32), (8, OLD // 8)).astype(BF)
    level = dot(level8, one_hot(iota((OLD // 8, OLD), 0) == iota((OLD // 8, OLD), 1) // 8))[0:1]

    rows8 = jnp.concatenate(
        [count, back, width, jnp.zeros((13, OLD), F32)], axis=0
    ).astype(BF)
    row_id, col_id = iota((OLD, OLD), 0), iota((OLD, OLD), 1)
    sums_col = dot_rows(one_hot(col_id < row_id), rows8)
    same_col = dot_rows(one_hot(col_id == row_id), rows8)
    sums_row = dot(rows8, one_hot(row_id < col_id))[0:1]
    start_col = sums_col[:, 0:1] - same_col[:, 1:2]
    end_col = start_col + same_col[:, 2:3]
    target = iota((1, WIDE), 1).astype(F32)
    chosen = one_hot((target >= start_col) & (target < end_col))

    parts = apply_beside(coarsen_ref[...], x)
    restricted = jnp.where(first, parts[0:64], 0.0)
    for k in range(1, 8):
        restricted = restricted + jnp.where(child == k, parts[64 * k : 64 * k + 64], 0.0)
    source = jnp.where(merged, restricted, x)
    high, low = split(source)
    refined = jnp.where(flag == 1, 1.0, 0.0)
    new_level = level + refined - jnp.where(merged, 1.0, 0.0)
    coarse_start = jnp.floor(sums_row * 0.0625)
    fine_start = sums_row - 16.0 * coarse_start
    info = jnp.concatenate([coarse_start, fine_start, new_level, refined], axis=0)
    info = jnp.where(merged & ~first, 0.0, info)
    info = jnp.concatenate([info, jnp.zeros((12, OLD), F32)], axis=0).astype(BF)
    picked = dot(jnp.concatenate([high, low, info], axis=0), chosen)
    record = picked[0:64] + picked[64:128]
    place = target - 16.0 * picked[128:129] - picked[129:130]
    is_refined = picked[131:132] > 0.5
    outs = apply_beside(refine_ref[...], record)
    fine = jnp.where(place == 0.0, outs[0:64], 0.0)
    for k in range(1, 8):
        fine = fine + jnp.where(place == float(k), outs[64 * k : 64 * k + 64], 0.0)
    cells = jnp.where(is_refined, fine, record)
    cells = jnp.concatenate([cells, jnp.broadcast_to(picked[130:131], (8, WIDE))], axis=0)
    cells_ref[...] = cells
    head = cells[:, 0:128]
    total = jnp.sum(count).astype(jnp.int32)
    tail = pltpu.roll(cells, (MOST - total) & (WIDE - 1), 1)[:, 0:128]
    even = lax.axis_index("sub") % 2 == 0
    pair_ref[...] = jnp.where(even, tail, head)
    other_ref[...] = jnp.where(even, head, tail)


def request(flag_ref, face_ref, code_ref, out_ref, slot_ref):
    flag = flag_ref[...]
    first = iota((1, OLD), 1) % 8 == 0
    count = jnp.where(flag == 1, 8.0, jnp.where((flag == 2) & ~first, 0.0, 1.0))
    produced = jnp.broadcast_to(jnp.sum(count, axis=1, keepdims=True), (GROUP, SLOTS))
    codes = code_ref[...]
    ghost = jnp.where(codes == 9, -1, face_ref[...] - NEW)
    cell = iota((1, NEW), 1)
    cell_high = (cell // 16).astype(F32)
    cell_low = (cell % 16).astype(F32)
    peers = iota((SUBS, NEW), 0)
    slots = iota((SLOTS, NEW), 0)
    info = jnp.zeros((4 * SUBS, SLOTS), F32)
    for face in range(6):
        entry = ghost[face : face + 1]
        named = (peers == entry // SLOTS) & (entry >= 0)
        code = codes[face : face + 1].astype(F32)
        rows = [jnp.where(named, value, 0.0) for value in (float(face), code, cell_high, cell_low)]
        info = info + dot_rows(
            jnp.concatenate(rows, axis=0).astype(BF), one_hot(slots == entry % SLOTS)
        )
    slot_ref[0:SUBS] = info[0:SUBS]
    slot_ref[SUBS : 2 * SUBS] = info[2 * SUBS : 3 * SUBS] * 16.0 + info[3 * SUBS : 4 * SUBS]
    slot_ref[2 * SUBS : 3 * SUBS] = info[SUBS : 2 * SUBS]
    out_ref[:, 0, 0:SLOTS] = produced
    out_ref[:, 0, SLOTS : 2 * SLOTS] = jnp.concatenate([info[0:SUBS]] * (GROUP // SUBS), axis=0)


def fetch(sources, landed, sems):
    copies = []
    for source, target in zip(sources, landed):
        rows = source.shape[0]
        pieces = PIECES if rows == 8 * 64 else 1
        for piece in range(pieces):
            part = pl.ds(piece * rows // pieces, rows // pieces)
            copies.append(
                pltpu.make_async_copy(source.at[part], target.at[part], sems.at[len(copies)])
            )
    for copy in copies:
        copy.start()
    for copy in copies:
        copy.wait()


def request_kernel(flag_hbm, face_hbm, code_hbm, asked_ref, slot_ref, *scratch):
    fetch((flag_hbm, face_hbm, code_hbm), scratch[:-1], scratch[-1])
    request(*scratch[:-1], asked_ref, slot_ref)


def expand_kernel(
    x_hbm, flag_hbm, level_hbm, coarsen_hbm, refine_hbm, cells_ref, pair_ref, other_ref, *scratch
):
    fetch((x_hbm, flag_hbm, level_hbm, coarsen_hbm, refine_hbm), scratch[:-1], scratch[-1])
    expand(*scratch[:-1], cells_ref, pair_ref, other_ref)


def total_kernel(near_ref, out_ref):
    total = jnp.sum(near_ref[:, 0:SLOTS], axis=0, keepdims=True)
    for place in range(out_ref.shape[0]):
        out_ref[place] = total


def choose_kernel(send_ref, out_ref):
    source = iota((PAD, SLOTS), 0)
    for peer in range(SUBS):
        out_ref[:, peer * SLOTS : (peer + 1) * SLOTS] = one_hot(source == send_ref[peer : peer + 1, :])


def place_kernel(
    ids_ref,
    near_ref,
    far_ref,
    cells_ref,
    met_ref,
    crossed_ref,
    chosen_ref,
    traces_ref,
    new_ref,
    pad_ref,
    trace_ref,
    out_ref,
):
    near = near_ref[:, 0:SLOTS]
    place = iota(near.shape, 0)
    inner = ids_ref[0]
    earlier = jnp.sum(jnp.where(place < inner, near, 0.0), axis=0, keepdims=True)
    own = jnp.sum(jnp.where(place == inner, near, 0.0), axis=0, keepdims=True)
    far = far_ref[...]
    earlier = earlier + jnp.sum(
        jnp.where(iota(far.shape, 0) < ids_ref[1], far, 0.0), axis=0, keepdims=True
    )
    shift = jnp.max(earlier).astype(jnp.int32) - ids_ref[2]
    end = shift + jnp.max(own).astype(jnp.int32)
    rolled = pltpu.roll(cells_ref[...], shift & (WIDE - 1), 1)
    even = lax.axis_index("sub") % 2 == 0
    met, crossed = met_ref[...], crossed_ref[...]
    before = pltpu.roll(jnp.where(even, crossed, met), (shift - MOST) & 127, 1)
    after = pltpu.roll(jnp.where(even, met, crossed), end & 127, 1)
    lane = iota((1, 128), 1)
    cells = jnp.concatenate(
        [
            jnp.where(lane < shift, before, rolled[:, 0:128]),
            rolled[:, 128:256],
            jnp.where(lane + 256 >= end, after, rolled[:, 256:384]),
        ],
        axis=1,
    )
    new_ref[...] = cells[0:64, 0:NEW]
    pad_ref[...] = cells
    high, low = split(apply_triple(traces_ref[...], cells[0:64]))
    both = jnp.concatenate([high, low], axis=0)
    trace_ref[...] = both
    mine = place // SUBS == ids_ref[3]
    rows = jnp.where(mine, near_ref[:, SLOTS : 2 * SLOTS], 0.0)
    wanted = rows[0:SUBS]
    for other in range(1, GROUP // SUBS):
        wanted = wanted + rows[other * SUBS : (other + 1) * SUBS]
    sent = dot(both, chosen_ref[...])
    for peer in range(SUBS):
        lanes = slice(peer * SLOTS, (peer + 1) * SLOTS)
        face = wanted[peer : peer + 1]
        picked = sent[0:16, lanes] + sent[96:112, lanes]
        for value in range(1, 6):
            rows = slice(16 * value, 16 * value + 16)
            lower = slice(96 + 16 * value, 112 + 16 * value)
            picked = jnp.where(face == float(value), sent[rows, lanes] + sent[lower, lanes], picked)
        out_ref[peer] = picked


def inside_kernel(
    pad_ref, trace_ref, face_ref, code_ref, volume_ref, lifts_ref, slot_ref, out_ref, owned_ref
):
    owner = iota((PAD, SLOTS), 0)
    for peer in range(SUBS):
        cell = slot_ref[SUBS + peer : SUBS + peer + 1].astype(jnp.int32)
        owned_ref[:, peer * SLOTS : (peer + 1) * SLOTS] = one_hot(owner == cell)
    traces = trace_ref[...]
    source = iota((PAD, NEW), 0)
    face_list = face_ref[...]
    face_list = jnp.where(face_list >= NEW, -1, face_list)
    codes = code_ref[...]
    highs, lows = [], []
    for face in range(6):
        both = jnp.concatenate(
            [traces[16 * face : 16 * face + 16], traces[96 + 16 * face : 112 + 16 * face]], axis=0
        )
        far = dot(both, one_hot(source == face_list[face : face + 1]))
        code = codes[face : face + 1]
        for value in range(9):
            kept = jnp.where(code == value, far, 0.0).astype(BF)
            highs.append(kept[0:16])
            lows.append(kept[16:32])
    lifts = lifts_ref[...]
    upper = dot(lifts, jnp.concatenate(highs, axis=0))
    lower = dot(lifts[0:64], jnp.concatenate(lows, axis=0))
    body = apply_triple(volume_ref[...], pad_ref[0:64, 0:NEW])
    out_ref[...] = body + upper[0:64] + upper[64:128] + lower


def outside_kernel(pad_ref, base_ref, ghost_ref, slot_ref, owned_ref, maps_ref, lifts_ref, out_ref):
    ghosts = jnp.concatenate([ghost_ref[peer] for peer in range(SUBS)], axis=1)
    mapped = apply_triple(maps_ref[...], ghosts)
    highs, lows = [], []
    for peer in range(SUBS):
        lanes = slice(peer * SLOTS, (peer + 1) * SLOTS)
        code = slot_ref[2 * SUBS + peer : 2 * SUBS + peer + 1]
        trace = mapped[0:16, lanes]
        for value in range(1, 9):
            rows = slice(16 * value, 16 * value + 16)
            trace = jnp.where(code == float(value), mapped[rows, lanes], trace)
        high, low = split(trace)
        both = jnp.concatenate([high.astype(F32), low.astype(F32)], axis=0)
        face = slot_ref[peer : peer + 1]
        kept = [jnp.where(face == float(value), both, 0.0).astype(BF) for value in range(6)]
        highs.append(jnp.concatenate([part[0:16] for part in kept], axis=0))
        lows.append(jnp.concatenate([part[16:32] for part in kept], axis=0))
    lifts = lifts_ref[...]
    upper = dot(lifts, jnp.concatenate(highs, axis=1))
    lower = dot(lifts[0:64], jnp.concatenate(lows, axis=1))
    high, low = split(upper[0:64] + upper[64:128] + lower)
    landed = dot_rows(jnp.concatenate([high, low], axis=0), owned_ref[...])
    result = base_ref[...] + (landed[0:64] + landed[64:128])[:, 0:NEW]
    level = pad_ref[64:65, 0:NEW]
    scale = jnp.zeros((1, NEW), F32)
    for value in range(LOW - 1, HIGH + 2):
        scale = jnp.where(level == float(value), 2.0 ** (LOW + 1 - value), scale)
    out_ref[...] = result * scale


def whole():
    return pl.BlockSpec(memory_space=pltpu.VMEM)


def shape(*dims, dtype=F32):
    return jax.ShapeDtypeStruct(dims, dtype)


PARAMS = pltpu.CompilerParams(vmem_limit_bytes=48 * 1024 * 1024)


def call(kernel, out_shape, *operands, scalars=0):
    specs = [pl.BlockSpec(memory_space=pltpu.SMEM)] * scalars
    specs += [whole()] * (len(operands) - scalars)
    return pl.pallas_call(
        kernel,
        out_shape=out_shape,
        in_specs=specs,
        out_specs=jax.tree.map(lambda _: whole(), out_shape),
        compiler_params=PARAMS,
        name=kernel.__name__,
    )(*operands)


def swaps(first, size):
    lower = range(first, size - 1, 2)
    return [(i, i + 1) for i in lower] + [(i + 1, i) for i in lower]


def call_fetching(kernel, out_shape, *operands):
    return pl.pallas_call(
        kernel,
        out_shape=out_shape,
        in_specs=[pl.BlockSpec(memory_space=pltpu.HBM)] * len(operands),
        out_specs=jax.tree.map(lambda _: whole(), out_shape),
        scratch_shapes=[pltpu.VMEM(x.shape, x.dtype) for x in operands]
        + [pltpu.SemaphoreType.DMA((PIECES * len(operands),))],
        name=kernel.__name__,
    )(*operands)


def on_device(old_field, adapt_flag, family_level, face_list, face_code, send_list):
    sub = lax.axis_index("sub")
    column = lax.axis_index("xc")
    outer = lax.axis_index("z")
    inner = column * lax.axis_size("sub") + sub
    outer_size = lax.axis_size("z")
    ids = jnp.stack([inner, outer, (outer * GROUP + inner) * NEW, column]).astype(jnp.int32)
    flag = adapt_flag.reshape(1, OLD)

    asked, slots = call_fetching(
        request_kernel,
        (shape(GROUP, 1, 2 * SLOTS), shape(3 * SUBS, SLOTS)),
        flag,
        face_list,
        face_code,
    )
    cells, pair, other = call_fetching(
        expand_kernel,
        (shape(72, WIDE), shape(72, 128), shape(72, 128)),
        old_field,
        flag,
        family_level.reshape(1, OLD // 8),
        jnp.asarray(COARSEN),
        jnp.asarray(REFINE),
    )
    with jax.named_scope("counts_inner"):
        near = lax.all_to_all(asked, ("xc", "sub"), 0, 0, tiled=True).reshape(GROUP, 2 * SLOTS)
    with jax.named_scope("counts_outer"):
        sums = call(total_kernel, shape(outer_size, 1, SLOTS), near)
    everything = ("z", "xc", "sub")
    size = outer_size * GROUP
    pair, sums = lax.optimization_barrier((pair, sums))
    with jax.named_scope("curve_halo"):
        met = lax.ppermute(pair, everything, swaps(0, size))
        crossed = lax.ppermute(other, everything, swaps(1, size))
    with jax.named_scope("counts_outer"):
        far = lax.all_to_all(sums, "z", 0, 0, tiled=True).reshape(outer_size, SLOTS)

    chosen = call(choose_kernel, shape(PAD, SUBS * SLOTS, dtype=BF), send_list)
    new_field, padded, traces, outgoing = call(
        place_kernel,
        (
            shape(64, NEW),
            shape(72, PAD),
            shape(192, PAD, dtype=BF),
            shape(SUBS, 16, SLOTS),
        ),
        ids,
        near,
        far,
        cells,
        met,
        crossed,
        chosen,
        jnp.asarray(TRACES),
        scalars=1,
    )
    with jax.named_scope("ghosts"):
        ghosts = lax.all_to_all(outgoing, "sub", 0, 0, tiled=True)
    base, owned = call(
        inside_kernel,
        (shape(64, NEW), shape(PAD, SUBS * SLOTS, dtype=BF)),
        padded,
        traces,
        face_list,
        face_code,
        jnp.asarray(VOLUME),
        jnp.asarray(LIFTED_MAPS),
        slots,
    )
    applied = call(
        outside_kernel, shape(64, NEW), padded, base, ghosts, slots, owned, jnp.asarray(MAPS), jnp.asarray(LIFTS)
    )
    return (new_field, applied)


def solution(mesh):
    seg, sub = mesh.shape["seg"], mesh.shape["sub"]
    columns = GROUP // sub
    finer = Mesh(mesh.devices.reshape(seg // columns, columns, sub), ("z", "xc", "sub"))
    flat = ("z", "xc", "sub")
    row, cols = P(flat), P(None, flat)
    return jax.shard_map(
        on_device,
        mesh=finer,
        in_specs=(cols, row, row, cols, cols, cols),
        out_specs=(cols, cols),
        check_vma=False,
    )
```

```python
import math

import jax
import jax.numpy as jnp
import numpy as np
from jax import lax
from jax.experimental import pallas as pl
from jax.experimental.pallas import tpu as pltpu
from jax.sharding import Mesh
from jax.sharding import PartitionSpec as P

BF = jnp.bfloat16
F32 = jnp.float32
OLD = 256
NEW = 368
PAD = 384
WIDE = 512
SLOTS = 128
SUBS = 8
GROUP = 64
PIECES = 2
MOST = 28
LOW = 6
HIGH = 8
PENALTY = 4.0
GAUSS_HALF = (
    (0.1834346424956498, 0.362683783378362),
    (0.525532409916329, 0.3137066458778873),
    (0.7966664774136267, 0.2223810344533745),
    (0.9602898564975363, 0.1012285362903763),
)


def basis_value(degree, point):
    forms = (1.0, point, 0.5 * (3.0 * point * point - 1.0), 0.5 * (5.0 * point**3 - 3.0 * point))
    return forms[degree] * math.sqrt(degree + 0.5)


def basis_slope(degree, point):
    forms = (0.0, 1.0, 3.0 * point, 0.5 * (15.0 * point * point - 3.0))
    return forms[degree] * math.sqrt(degree + 0.5)


def legendre_tables():
    nodes = [(sign * point, weight) for point, weight in GAUSS_HALF for sign in (1.0, -1.0)]
    prolong = np.zeros((2, 4, 4))
    stiff = np.zeros((4, 4))
    edge = np.zeros((2, 4))
    for i in range(4):
        for j in range(4):
            for half in range(2):
                prolong[half, i, j] = sum(
                    w * basis_value(i, p) * basis_value(j, (p + 2.0 * half - 1.0) / 2.0)
                    for p, w in nodes
                )
            stiff[i, j] = sum(w * basis_slope(i, p) * basis_slope(j, p) for p, w in nodes)
        for side in range(2):
            edge[side, i] = basis_value(i, 2.0 * side - 1.0)
    return prolong, stiff, edge


def halves_of(weights):
    high = np.asarray(weights, np.float32).astype(jnp.bfloat16)
    low = (np.asarray(weights, np.float32) - high.astype(np.float32)).astype(jnp.bfloat16)
    return high, low


def triple(weights):
    high, low = halves_of(weights)
    return np.concatenate([high, low, high], axis=1)


def beside(weights):
    return np.concatenate(halves_of(weights), axis=1)


def double(weights):
    high, low = halves_of(weights)
    return np.concatenate([high, low], axis=0)


def build_tables():
    prolong, stiff, edge = legendre_tables()
    eye = np.eye(4)
    children = [(k // 4, k // 2 % 2, k % 2) for k in range(8)]
    refine = np.concatenate(
        [np.kron(np.kron(prolong[x], prolong[y]), prolong[z]) for x, y, z in children]
    )
    coarsen = np.concatenate(
        [
            0.125 * np.kron(np.kron(prolong[x].T, prolong[y].T), prolong[z].T)
            for x, y, z in children
        ]
    )

    def along(axis, matrix):
        parts = [eye, eye, eye]
        parts[axis] = matrix
        return np.kron(np.kron(parts[0], parts[1]), parts[2])

    maps = [np.eye(16)]
    maps.extend(np.kron(prolong[o // 2], prolong[o % 2]) for o in range(4))
    maps.extend(0.25 * np.kron(prolong[o // 2].T, prolong[o % 2].T) for o in range(4))
    volume = sum(along(axis, stiff) for axis in range(3))
    traces = []
    lifts = []
    for face in range(6):
        axis, side = face // 2, face % 2
        volume = volume + PENALTY * along(axis, np.outer(edge[side], edge[side]))
        traces.append(along(axis, edge[1 - side][None, :]))
        lifts.append(-PENALTY * along(axis, edge[side][:, None]))
    return (
        beside(coarsen),
        beside(refine),
        triple(np.concatenate(traces)),
        triple(np.concatenate(maps)),
        triple(volume),
        double(np.concatenate([lift @ m for lift in lifts for m in maps], axis=1)),
        double(np.concatenate(lifts, axis=1)),
    )


COARSEN, REFINE, TRACES, MAPS, VOLUME, LIFTED_MAPS, LIFTS = build_tables()


def dot(a, b):
    return jnp.dot(a, b, preferred_element_type=F32)


def dot_rows(a, b):
    return lax.dot_general(a, b, (((1,), (1,)), ((), ())), preferred_element_type=F32)


def split(x):
    high = x.astype(BF)
    return high, (x - high.astype(F32)).astype(BF)


def apply_triple(weights, x):
    high, low = split(x)
    return dot(weights, jnp.concatenate([high, high, low], axis=0))


def apply_beside(weights, x):
    high, low = split(x)
    return dot(weights, jnp.concatenate([high, high], axis=0)) + dot(weights[:, 0:64], low)


def iota(shape, axis):
    return lax.broadcasted_iota(jnp.int32, shape, axis)


def one_hot(mask):
    return jnp.where(mask, 1.0, 0.0).astype(BF)


def expand(x_ref, flag_ref, level_ref, coarsen_ref, refine_ref, cells_ref, pair_ref, other_ref):
    x = x_ref[...]
    flag = flag_ref[...]
    lane = iota((1, OLD), 1)
    child = lane % 8
    merged = flag == 2
    first = child == 0
    count = jnp.where(flag == 1, 8.0, jnp.where(merged, jnp.where(first, 1.0, 0.0), 1.0))
    back = jnp.where(merged & ~first, 1.0, 0.0)
    width = jnp.where(flag == 1, 8.0, 1.0)
    level8 = jnp.broadcast_to(level_ref[...].astype(F32), (8, OLD // 8)).astype(BF)
    level = dot(level8, one_hot(iota((OLD // 8, OLD), 0) == iota((OLD // 8, OLD), 1) // 8))[0:1]

    rows8 = jnp.concatenate(
        [count, back, width, jnp.zeros((13, OLD), F32)], axis=0
    ).astype(BF)
    row_id, col_id = iota((OLD, OLD), 0), iota((OLD, OLD), 1)
    sums_col = dot_rows(one_hot(col_id < row_id), rows8)
    same_col = dot_rows(one_hot(col_id == row_id), rows8)
    sums_row = dot(rows8, one_hot(row_id < col_id))[0:1]
    start_col = sums_col[:, 0:1] - same_col[:, 1:2]
    end_col = start_col + same_col[:, 2:3]
    target = iota((1, WIDE), 1).astype(F32)
    chosen = one_hot((target >= start_col) & (target < end_col))

    parts = apply_beside(coarsen_ref[...], x)
    restricted = jnp.where(first, parts[0:64], 0.0)
    for k in range(1, 8):
        restricted = restricted + jnp.where(child == k, parts[64 * k : 64 * k + 64], 0.0)
    source = jnp.where(merged, restricted, x)
    high, low = split(source)
    refined = jnp.where(flag == 1, 1.0, 0.0)
    new_level = level + refined - jnp.where(merged, 1.0, 0.0)
    coarse_start = jnp.floor(sums_row * 0.0625)
    fine_start = sums_row - 16.0 * coarse_start
    info = jnp.concatenate([coarse_start, fine_start, new_level, refined], axis=0)
    info = jnp.where(merged & ~first, 0.0, info)
    info = jnp.concatenate([info, jnp.zeros((12, OLD), F32)], axis=0).astype(BF)
    picked = dot(jnp.concatenate([high, low, info], axis=0), chosen)
    record = picked[0:64] + picked[64:128]
    place = target - 16.0 * picked[128:129] - picked[129:130]
    is_refined = picked[131:132] > 0.5
    outs = apply_beside(refine_ref[...], record)
    fine = jnp.where(place == 0.0, outs[0:64], 0.0)
    for k in range(1, 8):
        fine = fine + jnp.where(place == float(k), outs[64 * k : 64 * k + 64], 0.0)
    cells = jnp.where(is_refined, fine, record)
    cells = jnp.concatenate([cells, jnp.broadcast_to(picked[130:131], (8, WIDE))], axis=0)
    cells_ref[...] = cells
    head = cells[:, 0:128]
    total = jnp.sum(count).astype(jnp.int32)
    tail = pltpu.roll(cells, (MOST - total) & (WIDE - 1), 1)[:, 0:128]
    even = lax.axis_index("sub") % 2 == 0
    pair_ref[...] = jnp.where(even, tail, head)
    other_ref[...] = jnp.where(even, head, tail)


def request(flag_ref, face_ref, code_ref, out_ref, slot_ref):
    flag = flag_ref[...]
    first = iota((1, OLD), 1) % 8 == 0
    count = jnp.where(flag == 1, 8.0, jnp.where((flag == 2) & ~first, 0.0, 1.0))
    produced = jnp.broadcast_to(jnp.sum(count, axis=1, keepdims=True), (GROUP, SLOTS))
    codes = code_ref[...]
    ghost = jnp.where(codes == 9, -1, face_ref[...] - NEW)
    cell = iota((1, NEW), 1)
    cell_high = (cell // 16).astype(F32)
    cell_low = (cell % 16).astype(F32)
    peers = iota((SUBS, NEW), 0)
    slots = iota((SLOTS, NEW), 0)
    info = jnp.zeros((4 * SUBS, SLOTS), F32)
    for face in range(6):
        entry = ghost[face : face + 1]
        named = (peers == entry // SLOTS) & (entry >= 0)
        code = codes[face : face + 1].astype(F32)
        rows = [jnp.where(named, value, 0.0) for value in (float(face), code, cell_high, cell_low)]
        info = info + dot_rows(
            jnp.concatenate(rows, axis=0).astype(BF), one_hot(slots == entry % SLOTS)
        )
    slot_ref[0:SUBS] = info[0:SUBS]
    slot_ref[SUBS : 2 * SUBS] = info[2 * SUBS : 3 * SUBS] * 16.0 + info[3 * SUBS : 4 * SUBS]
    slot_ref[2 * SUBS : 3 * SUBS] = info[SUBS : 2 * SUBS]
    out_ref[:, 0, 0:SLOTS] = produced
    out_ref[:, 0, SLOTS : 2 * SLOTS] = jnp.concatenate([info[0:SUBS]] * (GROUP // SUBS), axis=0)


def fetch(sources, landed, sems):
    copies = []
    for source, target in zip(sources, landed):
        rows = source.shape[0]
        pieces = PIECES if rows == 8 * 64 else 1
        for piece in range(pieces):
            part = pl.ds(piece * rows // pieces, rows // pieces)
            copies.append(
                pltpu.make_async_copy(source.at[part], target.at[part], sems.at[len(copies)])
            )
    for copy in copies:
        copy.start()
    for copy in copies:
        copy.wait()


def request_kernel(flag_hbm, face_hbm, code_hbm, asked_ref, slot_ref, *scratch):
    fetch((flag_hbm, face_hbm, code_hbm), scratch[:-1], scratch[-1])
    request(*scratch[:-1], asked_ref, slot_ref)


def expand_kernel(
    x_hbm, flag_hbm, level_hbm, coarsen_hbm, refine_hbm, cells_ref, pair_ref, other_ref, *scratch
):
    fetch((x_hbm, flag_hbm, level_hbm, coarsen_hbm, refine_hbm), scratch[:-1], scratch[-1])
    expand(*scratch[:-1], cells_ref, pair_ref, other_ref)


def total_kernel(near_ref, out_ref):
    total = jnp.sum(near_ref[:, 0:SLOTS], axis=0, keepdims=True)
    for place in range(out_ref.shape[0]):
        out_ref[place] = total


def choose_kernel(send_ref, out_ref):
    source = iota((PAD, SLOTS), 0)
    for peer in range(SUBS):
        out_ref[:, peer * SLOTS : (peer + 1) * SLOTS] = one_hot(source == send_ref[peer : peer + 1, :])


def place_kernel(
    ids_ref,
    near_ref,
    far_ref,
    cells_ref,
    met_ref,
    crossed_ref,
    chosen_ref,
    traces_ref,
    pad_ref,
    trace_ref,
    out_ref,
):
    near = near_ref[:, 0:SLOTS]
    place = iota(near.shape, 0)
    inner = ids_ref[0]
    earlier = jnp.sum(jnp.where(place < inner, near, 0.0), axis=0, keepdims=True)
    own = jnp.sum(jnp.where(place == inner, near, 0.0), axis=0, keepdims=True)
    far = far_ref[...]
    earlier = earlier + jnp.sum(
        jnp.where(iota(far.shape, 0) < ids_ref[1], far, 0.0), axis=0, keepdims=True
    )
    shift = jnp.max(earlier).astype(jnp.int32) - ids_ref[2]
    end = shift + jnp.max(own).astype(jnp.int32)
    rolled = pltpu.roll(cells_ref[...], shift & (WIDE - 1), 1)
    even = lax.axis_index("sub") % 2 == 0
    met, crossed = met_ref[...], crossed_ref[...]
    before = pltpu.roll(jnp.where(even, crossed, met), (shift - MOST) & 127, 1)
    after = pltpu.roll(jnp.where(even, met, crossed), end & 127, 1)
    lane = iota((1, 128), 1)
    cells = jnp.concatenate(
        [
            jnp.where(lane < shift, before, rolled[:, 0:128]),
            rolled[:, 128:256],
            jnp.where(lane + 256 >= end, after, rolled[:, 256:384]),
        ],
        axis=1,
    )
    pad_ref[...] = cells
    high, low = split(apply_triple(traces_ref[...], cells[0:64]))
    both = jnp.concatenate([high, low], axis=0)
    trace_ref[...] = both
    mine = place // SUBS == ids_ref[3]
    rows = jnp.where(mine, near_ref[:, SLOTS : 2 * SLOTS], 0.0)
    wanted = rows[0:SUBS]
    for other in range(1, GROUP // SUBS):
        wanted = wanted + rows[other * SUBS : (other + 1) * SUBS]
    sent = dot(both, chosen_ref[...])
    for peer in range(SUBS):
        lanes = slice(peer * SLOTS, (peer + 1) * SLOTS)
        face = wanted[peer : peer + 1]
        picked = sent[0:16, lanes] + sent[96:112, lanes]
        for value in range(1, 6):
            rows = slice(16 * value, 16 * value + 16)
            lower = slice(96 + 16 * value, 112 + 16 * value)
            picked = jnp.where(face == float(value), sent[rows, lanes] + sent[lower, lanes], picked)
        out_ref[peer] = picked


def inside_kernel(
    pad_ref,
    trace_ref,
    face_ref,
    code_ref,
    volume_ref,
    lifts_ref,
    slot_ref,
    new_ref,
    out_ref,
    owned_ref,
):
    new_ref[...] = pad_ref[0:64, 0:NEW]
    owner = iota((PAD, SLOTS), 0)
    for peer in range(SUBS):
        cell = slot_ref[SUBS + peer : SUBS + peer + 1].astype(jnp.int32)
        owned_ref[:, peer * SLOTS : (peer + 1) * SLOTS] = one_hot(owner == cell)
    traces = trace_ref[...]
    source = iota((PAD, NEW), 0)
    face_list = face_ref[...]
    face_list = jnp.where(face_list >= NEW, -1, face_list)
    codes = code_ref[...]
    highs, lows = [], []
    for face in range(6):
        both = jnp.concatenate(
            [traces[16 * face : 16 * face + 16], traces[96 + 16 * face : 112 + 16 * face]], axis=0
        )
        far = dot(both, one_hot(source == face_list[face : face + 1]))
        code = codes[face : face + 1]
        for value in range(9):
            kept = jnp.where(code == value, far, 0.0).astype(BF)
            highs.append(kept[0:16])
            lows.append(kept[16:32])
    lifts = lifts_ref[...]
    upper = dot(lifts, jnp.concatenate(highs, axis=0))
    lower = dot(lifts[0:64], jnp.concatenate(lows, axis=0))
    body = apply_triple(volume_ref[...], pad_ref[0:64, 0:NEW])
    out_ref[...] = body + upper[0:64] + upper[64:128] + lower


def outside_kernel(pad_ref, base_ref, ghost_ref, slot_ref, owned_ref, maps_ref, lifts_ref, out_ref):
    ghosts = jnp.concatenate([ghost_ref[peer] for peer in range(SUBS)], axis=1)
    mapped = apply_triple(maps_ref[...], ghosts)
    highs, lows = [], []
    for peer in range(SUBS):
        lanes = slice(peer * SLOTS, (peer + 1) * SLOTS)
        code = slot_ref[2 * SUBS + peer : 2 * SUBS + peer + 1]
        trace = mapped[0:16, lanes]
        for value in range(1, 9):
            rows = slice(16 * value, 16 * value + 16)
            trace = jnp.where(code == float(value), mapped[rows, lanes], trace)
        high, low = split(trace)
        both = jnp.concatenate([high.astype(F32), low.astype(F32)], axis=0)
        face = slot_ref[peer : peer + 1]
        kept = [jnp.where(face == float(value), both, 0.0).astype(BF) for value in range(6)]
        highs.append(jnp.concatenate([part[0:16] for part in kept], axis=0))
        lows.append(jnp.concatenate([part[16:32] for part in kept], axis=0))
    lifts = lifts_ref[...]
    upper = dot(lifts, jnp.concatenate(highs, axis=1))
    lower = dot(lifts[0:64], jnp.concatenate(lows, axis=1))
    high, low = split(upper[0:64] + upper[64:128] + lower)
    landed = dot_rows(jnp.concatenate([high, low], axis=0), owned_ref[...])
    result = base_ref[...] + (landed[0:64] + landed[64:128])[:, 0:NEW]
    level = pad_ref[64:65, 0:NEW]
    scale = jnp.zeros((1, NEW), F32)
    for value in range(LOW - 1, HIGH + 2):
        scale = jnp.where(level == float(value), 2.0 ** (LOW + 1 - value), scale)
    out_ref[...] = result * scale


def whole():
    return pl.BlockSpec(memory_space=pltpu.VMEM)


def shape(*dims, dtype=F32):
    return jax.ShapeDtypeStruct(dims, dtype)


PARAMS = pltpu.CompilerParams(vmem_limit_bytes=48 * 1024 * 1024)


def call(kernel, out_shape, *operands, scalars=0):
    specs = [pl.BlockSpec(memory_space=pltpu.SMEM)] * scalars
    specs += [whole()] * (len(operands) - scalars)
    return pl.pallas_call(
        kernel,
        out_shape=out_shape,
        in_specs=specs,
        out_specs=jax.tree.map(lambda _: whole(), out_shape),
        compiler_params=PARAMS,
        name=kernel.__name__,
    )(*operands)


def swaps(first, size):
    lower = range(first, size - 1, 2)
    return [(i, i + 1) for i in lower] + [(i + 1, i) for i in lower]


def call_fetching(kernel, out_shape, *operands):
    return pl.pallas_call(
        kernel,
        out_shape=out_shape,
        in_specs=[pl.BlockSpec(memory_space=pltpu.HBM)] * len(operands),
        out_specs=jax.tree.map(lambda _: whole(), out_shape),
        scratch_shapes=[pltpu.VMEM(x.shape, x.dtype) for x in operands]
        + [pltpu.SemaphoreType.DMA((PIECES * len(operands),))],
        name=kernel.__name__,
    )(*operands)


def on_device(old_field, adapt_flag, family_level, face_list, face_code, send_list):
    sub = lax.axis_index("sub")
    column = lax.axis_index("xc")
    outer = lax.axis_index("z")
    inner = column * lax.axis_size("sub") + sub
    outer_size = lax.axis_size("z")
    ids = jnp.stack([inner, outer, (outer * GROUP + inner) * NEW, column]).astype(jnp.int32)
    flag = adapt_flag.reshape(1, OLD)

    asked, slots = call_fetching(
        request_kernel,
        (shape(GROUP, 1, 2 * SLOTS), shape(3 * SUBS, SLOTS)),
        flag,
        face_list,
        face_code,
    )
    cells, pair, other = call_fetching(
        expand_kernel,
        (shape(72, WIDE), shape(72, 128), shape(72, 128)),
        old_field,
        flag,
        family_level.reshape(1, OLD // 8),
        jnp.asarray(COARSEN),
        jnp.asarray(REFINE),
    )
    with jax.named_scope("counts_inner"):
        near = lax.all_to_all(asked, ("xc", "sub"), 0, 0, tiled=True).reshape(GROUP, 2 * SLOTS)
    with jax.named_scope("counts_outer"):
        sums = call(total_kernel, shape(outer_size, 1, SLOTS), near)
    everything = ("z", "xc", "sub")
    size = outer_size * GROUP
    pair, sums = lax.optimization_barrier((pair, sums))
    with jax.named_scope("curve_halo"):
        met = lax.ppermute(pair, everything, swaps(0, size))
        crossed = lax.ppermute(other, everything, swaps(1, size))
    with jax.named_scope("counts_outer"):
        far = lax.all_to_all(sums, "z", 0, 0, tiled=True).reshape(outer_size, SLOTS)

    chosen = call(choose_kernel, shape(PAD, SUBS * SLOTS, dtype=BF), send_list)
    padded, traces, outgoing = call(
        place_kernel,
        (
            shape(72, PAD),
            shape(192, PAD, dtype=BF),
            shape(SUBS, 16, SLOTS),
        ),
        ids,
        near,
        far,
        cells,
        met,
        crossed,
        chosen,
        jnp.asarray(TRACES),
        scalars=1,
    )
    with jax.named_scope("ghosts"):
        ghosts = lax.all_to_all(outgoing, "sub", 0, 0, tiled=True)
    new_field, base, owned = call(
        inside_kernel,
        (shape(64, NEW), shape(64, NEW), shape(PAD, SUBS * SLOTS, dtype=BF)),
        padded,
        traces,
        face_list,
        face_code,
        jnp.asarray(VOLUME),
        jnp.asarray(LIFTED_MAPS),
        slots,
    )
    applied = call(
        outside_kernel, shape(64, NEW), padded, base, ghosts, slots, owned, jnp.asarray(MAPS), jnp.asarray(LIFTS)
    )
    return (new_field, applied)


def solution(mesh):
    seg, sub = mesh.shape["seg"], mesh.shape["sub"]
    columns = GROUP // sub
    finer = Mesh(mesh.devices.reshape(seg // columns, columns, sub), ("z", "xc", "sub"))
    flat = ("z", "xc", "sub")
    row, cols = P(flat), P(None, flat)
    return jax.shard_map(
        on_device,
        mesh=finer,
        in_specs=(cols, row, row, cols, cols, cols),
        out_specs=(cols, cols),
        check_vma=False,
    )
```
